32 devices in a mesh: dom: 16 (over z, x, core), sub: 2 (over y).
Axes of the slice: x: 2, y: 2, z: 4, core: 2. Of those that a mesh axis runs over, the one named last changes fastest.
Arguments:
- node_features: bfloat16 [65536, 128], P(('dom', 'sub')), may hold values from -6 to 6
- near_fine: int32 [512, 3], P(('dom', 'sub')), may hold values from 0 to 511, as said below
- near_mid: int32 [128, 3], replicated, may hold values from 0 to 127, as said below
- near_top: int32 [32, 3], replicated, may hold values from 0 to 31, as said below
- restrict_mid: int32 [128, 4], replicated, may hold values from 0 to 511, as said below
- restrict_top: int32 [32, 4], replicated, may hold values from 0 to 127, as said below
- node_kernel: bfloat16 [3, 3, 128, 128], replicated, may hold values from -0.5 to 0.5
- channel_kernel: bfloat16 [3, 3, 128, 128], replicated, may hold values from -0.3125 to 0.3125
- restrict_weight: bfloat16 [2, 4, 128, 128], replicated, may hold values from -0.25 to 0.25
- interp_weight: bfloat16 [2, 4, 128, 128], replicated, may hold values from -0.5 to 0.5
- skip_weight: bfloat16 [128, 128], replicated, may hold values from -0.5 to 0.5
Outputs:
- updated: bfloat16 [65536, 128], P(('dom', 'sub'))
The draws below stay inside these ranges and needn't reach their ends.
Inputs may be any that keep to these rules, and one draw needn't show every extreme that they name: `near_fine`: blocks are numbered region by region along dom+sub, 16 to a device. Row i names in column 0 a block of the same device, in column 1 one of the last 4 blocks of the previous device and in column 2 one of the first 4 blocks of the next device; where that device does not exist, a block of the same device. `near_mid`: A middle-level group is the 16 blocks numbered g * 16 to (g + 1) * 16 - 1 with g = D * 2 + s, D < 16 // 4. Row i of group (D, s) names in column 0 a block of its group, in column 1 one of the last 4 blocks of group (D - 1, s) and in column 2 one of the first 4 blocks of group (D + 1, s); where that group does not exist, a block of its own group. `near_top`: as for near_mid, with groups (D, s), D < 16 // 16, of the coarsest level. `restrict_mid`: row j = (D * 2 + s) * 16 + b lists, in some order, the four blocks ((4 D + r) * 2 + s) * 16 + b for r = 0..3 of the finest level. `restrict_top`: row j = (D * 2 + s) * 16 + b lists, in some order, the four blocks ((4 D + r) * 2 + s) * 16 + b for r = 0..3 of the middle level.
All inputs are finite; a program needn't handle non-finite values.
Results may differ from the reference program's by a relative error of at most 0.0075.
Values may be sent and summed in bfloat16 or wider, within the bound.
A program may use at most 64 MiB of HBM per device.

```python
import jax
import jax.numpy as jnp

C = 128
BS = 128
KN = 3
LEVELS = 3
BLK_DEV = 16
HALO_BLK = 4
B0 = 512
NODES = 65536
N_DOM = 16
N_SUB = 2
DEVICES = 32


def near_pattern(key, tier_index):
    blocks_total = B0 // 4 ** tier_index
    block_ids = jnp.arange(blocks_total, dtype=jnp.int32)
    group_of = block_ids // BLK_DEV
    if tier_index == 0:
        step_groups = 1
        has_lower = group_of > 0
        has_upper = group_of < DEVICES - 1
    else:
        step_groups = N_SUB
        dom_group = group_of // N_SUB
        has_lower = dom_group > 0
        has_upper = dom_group < N_DOM // 4 ** tier_index - 1
    key_own, key_spare, key_extra, key_lower, key_upper = jax.random.split(key, 5)
    own_pick = group_of * BLK_DEV + jax.random.randint(key_own, (blocks_total,), 0, BLK_DEV, dtype=jnp.int32)
    spare_one = group_of * BLK_DEV + jax.random.randint(key_spare, (blocks_total,), 0, BLK_DEV, dtype=jnp.int32)
    spare_two = group_of * BLK_DEV + jax.random.randint(key_extra, (blocks_total,), 0, BLK_DEV, dtype=jnp.int32)
    lower_pick = (group_of - step_groups) * BLK_DEV + BLK_DEV - HALO_BLK + jax.random.randint(key_lower, (blocks_total,), 0, HALO_BLK, dtype=jnp.int32)
    upper_pick = (group_of + step_groups) * BLK_DEV + jax.random.randint(key_upper, (blocks_total,), 0, HALO_BLK, dtype=jnp.int32)
    column_one = jnp.where(has_lower, lower_pick, spare_one)
    column_two = jnp.where(has_upper, upper_pick, spare_two)
    return jnp.stack([own_pick, column_one, column_two], axis=1).astype(jnp.int32)


def child_pattern(key, tier_index):
    blocks_total = B0 // 4 ** tier_index
    block_ids = jnp.arange(blocks_total, dtype=jnp.int32)
    group_of = block_ids // BLK_DEV
    inner_pos = block_ids % BLK_DEV
    dom_group = group_of // N_SUB
    sub_part = group_of % N_SUB
    children = jnp.stack([((4 * dom_group + quarter) * N_SUB + sub_part) * BLK_DEV + inner_pos for quarter in range(4)], axis=1)
    scores = jax.random.randint(key, (blocks_total, 4), 0, 2 ** 20, dtype=jnp.int32) * 4 + jnp.arange(4, dtype=jnp.int32)
    ranking = jnp.argsort(scores, axis=1, stable=True)
    return jnp.take_along_axis(children, ranking, axis=1).astype(jnp.int32)


def draw_near_fine(key, part):
    return near_pattern(jax.random.fold_in(key, 11), 0)


def draw_near_mid(key, part):
    return near_pattern(jax.random.fold_in(key, 12), 1)


def draw_near_top(key, part):
    return near_pattern(jax.random.fold_in(key, 13), 2)


def draw_restrict_mid(key, part):
    return child_pattern(jax.random.fold_in(key, 21), 1)


def draw_restrict_top(key, part):
    return child_pattern(jax.random.fold_in(key, 22), 2)


def shard_levels(rng, extent, cuts, smallest, top_value):
    level = 1.0
    for dim, blocks in cuts:
        draws = jax.random.uniform(jax.random.fold_in(jax.random.fold_in(rng, 6), dim), (blocks,), jnp.float32, smallest / len(cuts), top_value / len(cuts))
        level = level * jnp.repeat(jnp.exp(draws), extent[dim] // blocks).reshape((-1,) + (1,) * (len(extent) - 1 - dim))
    return level


def centred(rng, dims, width, bound, shards=(), kind=jnp.bfloat16):
    entries = width * jax.random.normal(rng, dims, jnp.float32)
    if shards:
        entries = entries * shard_levels(rng, dims, shards, -0.22, 0.18)
    return jnp.clip(entries, -bound, bound).astype(kind)


def setup_inputs(seed: int = 0) -> dict:
    keys = jax.random.split(jax.random.key(seed), 12)
    node_features = centred(keys[0], (NODES, C), 1.0, 6.0, ((0, 32),))
    near_fine = draw_near_fine(jax.random.fold_in(keys[11], 71), 0)
    near_mid = draw_near_mid(jax.random.fold_in(keys[11], 71), 0)
    near_top = draw_near_top(jax.random.fold_in(keys[11], 71), 0)
    restrict_mid = draw_restrict_mid(jax.random.fold_in(keys[11], 71), 0)
    restrict_top = draw_restrict_top(jax.random.fold_in(keys[11], 71), 0)
    node_kernel = centred(keys[6], (LEVELS, KN, BS, BS), BS ** -0.5, 0.5)
    channel_kernel = centred(keys[7], (LEVELS, KN, C, C), (KN * C) ** -0.5, 0.3125)
    restrict_weight = centred(keys[8], (LEVELS - 1, 4, BS, BS), (4 * BS) ** -0.5, 0.25)
    interp_weight = centred(keys[9], (LEVELS - 1, 4, BS, BS), BS ** -0.5, 0.5)
    skip_weight = centred(keys[10], (C, C), C ** -0.5, 0.5)
    return {"node_features": node_features, "near_fine": near_fine, "near_mid": near_mid, "near_top": near_top, "restrict_mid": restrict_mid, "restrict_top": restrict_top, "node_kernel": node_kernel, "channel_kernel": channel_kernel, "restrict_weight": restrict_weight, "interp_weight": interp_weight, "skip_weight": skip_weight}


def near_level(values, near_rows, node_mats, chan_mats):
    flat_rows = values.reshape(-1, C)
    summed = jnp.zeros(values.shape, jnp.float32)
    for column in range(KN):
        mixed_rows = jnp.dot(flat_rows, chan_mats[column], preferred_element_type=jnp.float32).astype(jnp.bfloat16).reshape(values.shape)
        picked = jnp.take(mixed_rows, near_rows[:, column], axis=0)
        summed = summed + jnp.einsum("pq,bqc->bpc", node_mats[column].astype(jnp.float32), picked.astype(jnp.float32))
    return summed


def restrict_level(values, kid_rows, matrices):
    summed = jnp.zeros((kid_rows.shape[0], BS, C), jnp.float32)
    for quarter in range(4):
        picked = jnp.take(values, kid_rows[:, quarter], axis=0)
        summed = summed + jnp.einsum("pq,bqc->bpc", matrices[quarter].astype(jnp.float32), picked.astype(jnp.float32))
    return summed.astype(jnp.bfloat16)


def interp_level(coarse, kid_rows, matrices, fine_count):
    added = jnp.zeros((fine_count, BS, C), jnp.float32)
    for quarter in range(4):
        values = jnp.einsum("pq,bqc->bpc", matrices[quarter].astype(jnp.float32), coarse.astype(jnp.float32))
        added = added.at[kid_rows[:, quarter]].add(values)
    return added


def reference(node_features, near_fine, near_mid, near_top, restrict_mid, restrict_top, node_kernel, channel_kernel, restrict_weight, interp_weight, skip_weight):
    near_lists = [near_fine, near_mid, near_top]
    kid_lists = [restrict_mid, restrict_top]
    levels_values = [node_features.reshape(-1, BS, C)]
    for tier_index in range(LEVELS - 1):
        levels_values.append(restrict_level(levels_values[tier_index], kid_lists[tier_index], restrict_weight[tier_index]))
    upward = near_level(levels_values[LEVELS - 1], near_lists[LEVELS - 1], node_kernel[LEVELS - 1], channel_kernel[LEVELS - 1])
    for tier_index in range(LEVELS - 2, -1, -1):
        coarse = upward.astype(jnp.bfloat16)
        near_part = near_level(levels_values[tier_index], near_lists[tier_index], node_kernel[tier_index], channel_kernel[tier_index])
        upward = near_part + interp_level(coarse, kid_lists[tier_index], interp_weight[tier_index], levels_values[tier_index].shape[0])
    skip_term = jnp.dot(node_features, skip_weight, preferred_element_type=jnp.float32)
    return jax.nn.gelu(skip_term + upward.reshape(-1, C)).astype(jnp.bfloat16)
```

```python
import functools

import jax
import jax.numpy as jnp
from jax import lax
from jax.experimental import pallas as pl
from jax.experimental.pallas import tpu as pltpu
from jax.sharding import PartitionSpec as P

C = 128
BS = 128
KN = 3
BLK = 16
HALO = 4
HALF = BLK // 2
QTR = BLK // 4
F32 = jnp.float32
BF16 = jnp.bfloat16
MESH = pl.DeviceIdType.MESH
FORWARD = 4


def dot(a, b):
    return jnp.dot(a, b, preferred_element_type=F32)


def gelu(x):
    inner = 0.7978845608028654 * (x + 0.044715 * (x * x * x))
    return 0.5 * x * (1.0 + jnp.tanh(inner))


def kernel(
    n_dom,
    n_sub,
    feat_h,
    nf_h,
    nm_h,
    nt_h,
    rm_h,
    rt_h,
    nk_h,
    ck_h,
    rw_h,
    iw_h,
    sk_h,
    out_h,
    v0,
    nk,
    ck,
    rw,
    iw,
    sk,
    nf,
    nm,
    nt,
    rm,
    rt,
    h0,
    r1,
    ps,
    pf,
    pr,
    v1w,
    zr,
    v2w,
    y0,
    y1,
    y2,
    u0,
    u1,
    ob,
    in_sem,
    out_sem,
    core_sem,
    fine_sem,
    part_sem,
    zs_sem,
    v1x_sem,
    v1c_sem,
    rim_sem,
    rimc_sem,
    v2z_sem,
    v2x_sem,
    v2c_sem,
    v2r_sem,
):
    dom = lax.axis_index("dom")
    sub = lax.axis_index("sub")
    n1 = n_dom // 4
    n2 = n_dom // 16
    g1 = dom // 4
    g2 = dom // 16
    r = dom % 4
    c = r % 2
    xb = r // 2
    zi = g1 % 4
    core_dom = dom + 1 - 2 * c
    x_dom = dom + 2 - 4 * xb
    q0 = c * HALF + xb * QTR
    qx = c * HALF + (1 - xb) * QTR
    start0 = (dom * n_sub + sub) * BLK
    start1 = (g1 * n_sub + sub) * BLK
    start2 = (g2 * n_sub + sub) * BLK
    me = dom * n_sub + sub
    prev_ok = me > 0
    next_ok = me < n_dom * n_sub - 1
    prev_dom = (me + n_dom * n_sub - 1) % (n_dom * n_sub) // n_sub
    prev_sub = (sub + n_sub - 1) % n_sub
    next_dom = (me + 1) % (n_dom * n_sub) // n_sub
    next_sub = (sub + 1) % n_sub
    prev1 = g1 > 0
    next1 = g1 < n1 - 1
    prev2 = g2 > 0
    next2 = g2 < n2 - 1
    is_c1 = c == 1
    is_c0 = c == 0

    def z_dom(k):
        return dom + ((zi + k) % 4 - zi) * 4

    loads = [
        pltpu.make_async_copy(feat_h, v0, in_sem.at[0]),
        pltpu.make_async_copy(rw_h, rw, in_sem.at[1]),
        pltpu.make_async_copy(rm_h, rm, in_sem.at[2]),
        pltpu.make_async_copy(rt_h, rt, in_sem.at[3]),
        pltpu.make_async_copy(ck_h, ck, in_sem.at[4]),
        pltpu.make_async_copy(sk_h, sk, in_sem.at[5]),
        pltpu.make_async_copy(nf_h, nf, in_sem.at[6]),
        pltpu.make_async_copy(nm_h, nm, in_sem.at[7]),
        pltpu.make_async_copy(nt_h, nt, in_sem.at[8]),
        pltpu.make_async_copy(nk_h, nk, in_sem.at[9]),
        pltpu.make_async_copy(iw_h, iw, in_sem.at[10]),
    ]
    for copy in loads:
        copy.start()

    barrier = pltpu.get_barrier_semaphore()

    def greet(d, s):
        pl.semaphore_signal(barrier, inc=1, device_id={"dom": d, "sub": s}, device_id_type=MESH)

    greet(core_dom, sub)
    greet(x_dom, sub)
    for k in range(1, 4):
        greet(z_dom(k), sub)
    both = [
        (prev_ok, prev_dom, prev_sub),
        (next_ok, next_dom, next_sub),
    ]
    if n1 > 4:
        both += [(prev1, dom - 4, sub), (next1, dom + 4, sub)]
    if n2 > 1:
        both += [(prev2, dom - 16, sub), (next2, dom + 16, sub)]
    for ok, d, s in both:
        @pl.when(ok)
        def _(d=d, s=s):
            greet(d, s)
    expected = 5
    for ok, _, _ in both:
        expected = expected + jnp.where(ok, 1, 0)
    pl.semaphore_wait(barrier, expected)

    def remote(src, dst, sems, i, d, s=None):
        return pltpu.make_async_remote_copy(
            src_ref=src,
            dst_ref=dst,
            send_sem=sems.at[0, i],
            recv_sem=sems.at[1, i],
            device_id={"dom": d, "sub": sub if s is None else s},
            device_id_type=MESH,
        )

    def own_slot(kids, b, ident):
        s = jnp.where(kids[1, b] == ident, 1, 0)
        s = jnp.where(kids[2, b] == ident, 2, s)
        return jnp.where(kids[3, b] == ident, 3, s)

    def fine_slot(d, b):
        return own_slot(rm, start1 + b, (d * n_sub + sub) * BLK + b)

    def mid_slot(k, b):
        return own_slot(rt, start2 + b, ((g2 * 4 + k) * n_sub + sub) * BLK + b)

    def local(near, own, pitch):
        lower = near - (own - pitch) - (BLK - HALO)
        upper = near - (own + pitch) + HALO + BLK
        mine = near - own + HALO
        window = jnp.where(near < own, lower, jnp.where(near >= own + BLK, upper, mine))
        return jnp.clip(window, 0, BLK + 2 * HALO - 1)

    loads[0].wait()
    core = remote(v0.at[pl.ds((1 - c) * HALF, HALF)], r1, core_sem, 0, core_dom)
    core.start()
    up = remote(v0.at[pl.ds(BLK - HALO, HALO)], h0.at[pl.ds(0, HALO)], fine_sem, 0, next_dom, next_sub)
    down = remote(v0.at[pl.ds(0, HALO)], h0.at[pl.ds(HALO, HALO)], fine_sem, 1, prev_dom, prev_sub)

    @pl.when(next_ok)
    def _():
        up.start()

    @pl.when(prev_ok)
    def _():
        down.start()

    for copy in loads[1:]:
        copy.wait()

    def maps(level, src, dst, first, at, count):
        wide = jnp.concatenate([ck[level, 0], ck[level, 1], ck[level, 2]], axis=1)
        rows = src[pl.ds(first, count)].reshape(count * BS, C)
        dst[pl.ds(at, count)] = dot(rows, wide).astype(BF16).reshape(count, BS, KN * C)

    def own_maps(i, _):
        rows = v0[pl.ds(i * 4, 4)].reshape(4 * BS, C)
        left = jnp.concatenate([ck[0, 0], ck[0, 1]], axis=1)
        right = jnp.concatenate([ck[0, 2], sk[...]], axis=1)
        y0[pl.ds(HALO + i * 4, 4), :, pl.ds(0, 2 * C)] = dot(rows, left).astype(BF16).reshape(4, BS, 2 * C)
        got = dot(rows, right)
        y0[pl.ds(HALO + i * 4, 4), :, pl.ds(2 * C, C)] = got[:, :C].astype(BF16).reshape(4, BS, C)
        u0[pl.ds(i * 4, 4)] = got[:, C:].reshape(4, BS, C)
        return 0

    lax.fori_loop(0, 4, own_maps, 0, unroll=True)

    core.wait_recv()

    def chip_sum(b):
        mats = jnp.concatenate([rw[0, fine_slot(dom, b)], rw[0, fine_slot(core_dom, b)]], axis=1)
        vals = jnp.concatenate([v0[b], r1[b - c * HALF]], axis=0)
        return dot(mats, vals)

    part = [remote(ps.at[i], pr.at[i], part_sem, i, x_dom) for i in range(QTR)]
    for i in range(QTR):
        ps[i] = chip_sum(qx + i).astype(BF16)
        part[i].start()
    for i in range(QTR):
        pf[i] = chip_sum(q0 + i)

    @pl.when(prev_ok)
    def _():
        down.wait_send()

    @pl.when(next_ok)
    def _():
        up.wait_send()

    @pl.when(prev_ok)
    def _():
        up.wait_recv()
        rows = h0[pl.ds(0, HALO)].reshape(HALO * BS, C)
        y0[pl.ds(0, HALO), :, pl.ds(C, C)] = dot(rows, ck[0, 1]).astype(BF16).reshape(HALO, BS, C)

    @pl.when(next_ok)
    def _():
        down.wait_recv()
        rows = h0[pl.ds(HALO, HALO)].reshape(HALO * BS, C)
        y0[pl.ds(HALO + BLK, HALO), :, pl.ds(2 * C, C)] = dot(rows, ck[0, 2]).astype(BF16).reshape(HALO, BS, C)

    def near_pair(level, y, near, first, own, pitch, i):
        mats = jnp.concatenate([nk[level, 0], nk[level, 1], nk[level, 2]], axis=1)
        sides = []
        for b in (2 * i, 2 * i + 1):
            picks = [
                y[local(near[k, first + b], own, pitch), :, pl.ds(k * C, C)] for k in range(KN)
            ]
            sides.append(jnp.concatenate(picks, axis=0))
        got = dot(mats, jnp.concatenate(sides, axis=1))
        return got[:, :C], got[:, C:]

    def near_fine(i, _):
        one, two = near_pair(0, y0, nf, 0, start0, BLK, i)
        u0[2 * i] += one
        u0[2 * i + 1] += two
        return 0

    lax.fori_loop(0, BLK // 2, near_fine, 0, unroll=True)

    zsend = [
        remote(v1w.at[HALO + q0 + (zi + k) % 4], zr.at[k - 1], zs_sem, k - 1, z_dom(k))
        for k in range(1, 4)
    ]
    for i in range(QTR):
        part[i].wait_recv()
        v1w[HALO + q0 + i] = (pf[i] + pr[i].astype(F32)).astype(BF16)
    for copy in (zsend[1], zsend[0], zsend[2]):
        copy.start()
    own_quarter = v1w.at[pl.ds(HALO + q0, QTR)]
    other_quarter = v1w.at[pl.ds(HALO + qx, QTR)]
    v1x = remote(own_quarter, own_quarter, v1x_sem, 0, x_dom)
    v1x.start()
    v1c = [
        remote(own_quarter, own_quarter, v1c_sem, 0, core_dom),
        remote(other_quarter, other_quarter, v1c_sem, 1, core_dom),
    ]
    v1c[0].start()

    b2 = q0 + zi
    mine = dot(rw[1, mid_slot(zi, b2)], v1w[HALO + b2])
    for copy in zsend:
        copy.wait_recv()
    mats = [rw[1, mid_slot((zi + 4 - k) % 4, b2)] for k in range(1, 4)]
    vals = [zr[k - 1] for k in range(1, 4)]
    mine = mine + dot(jnp.concatenate(mats, axis=1), jnp.concatenate(vals, axis=0))
    v2w[HALO + b2] = mine.astype(BF16)

    def block2(b):
        return v2w.at[HALO + b]

    v2z = [remote(block2(b2), block2(b2), v2z_sem, k - 1, z_dom(k)) for k in range(1, 4)]
    for copy in (v2z[1], v2z[0], v2z[2]):
        copy.start()
    hops = [(zi + 4 - k) % 4 for k in range(4)]
    v2x = [remote(block2(q0 + h), block2(q0 + h), v2x_sem, k, x_dom) for k, h in enumerate(hops)]
    v2c = [remote(block2(q0 + h), block2(q0 + h), v2c_sem, k, core_dom) for k, h in enumerate(hops)]
    v2c += [remote(block2(qx + h), block2(qx + h), v2c_sem, 4 + k, core_dom) for k, h in enumerate(hops)]
    v2x[0].start()
    v2c[0].start()

    v1x.wait_recv()
    v1c[1].start()
    low = v1w.at[pl.ds(0, HALO)]
    high = v1w.at[pl.ds(HALO + BLK, HALO)]
    rim_up = remote(v1w.at[pl.ds(BLK, HALO)], low, rim_sem, 0, jnp.minimum(dom + 4, n_dom - 1))
    rim_down = remote(v1w.at[pl.ds(HALO, HALO)], high, rim_sem, 1, jnp.maximum(dom - 4, 0))
    low_core = remote(low, low, rimc_sem, 0, core_dom)
    high_core = remote(high, high, rimc_sem, 1, core_dom)

    @pl.when(is_c1 & next1)
    def _():
        rim_up.start()

    @pl.when(is_c0 & prev1)
    def _():
        rim_down.start()

    v1c[0].wait_recv()
    v1c[1].wait_recv()

    def mid_maps(i, _):
        maps(1, v1w, y1, HALO + i * 4, HALO + i * 4, 4)
        return 0

    lax.fori_loop(0, 4, mid_maps, 0, unroll=True)

    for k in (1, 3, 2):
        v2z[k - 1].wait_recv()
        v2x[k].start()
        v2c[k].start()

    @pl.when(is_c1 & prev1)
    def _():
        rim_up.wait_recv()
        low_core.start()

    @pl.when(is_c0 & next1)
    def _():
        rim_down.wait_recv()
        high_core.start()

    @pl.when(is_c0 & prev1)
    def _():
        low_core.wait_recv()

    @pl.when(is_c1 & next1)
    def _():
        high_core.wait_recv()

    @pl.when(prev1)
    def _():
        rows = v1w[pl.ds(0, HALO)].reshape(HALO * BS, C)
        y1[pl.ds(0, HALO), :, pl.ds(C, C)] = dot(rows, ck[1, 1]).astype(BF16).reshape(HALO, BS, C)

    @pl.when(next1)
    def _():
        rows = v1w[pl.ds(HALO + BLK, HALO)].reshape(HALO * BS, C)
        y1[pl.ds(HALO + BLK, HALO), :, pl.ds(2 * C, C)] = dot(rows, ck[1, 2]).astype(BF16).reshape(HALO, BS, C)

    def near_mid(i, _):
        one, two = near_pair(1, y1, nm, start1, start1, n_sub * BLK, i)
        u1[2 * i] = one
        u1[2 * i + 1] = two
        return 0

    lax.fori_loop(0, BLK // 2 - FORWARD, near_mid, 0, unroll=True)
    for k in (0, 1, 3, 2):
        v2x[k].wait_recv()
        v2c[4 + k].start()
    lax.fori_loop(BLK // 2 - FORWARD, BLK // 2, near_mid, 0, unroll=True)

    maps(2, v2w, y2, HALO + c * HALF, HALO + c * HALF, HALF)
    for k in range(2 * QTR):
        v2c[k].wait_recv()
    maps(2, v2w, y2, HALO + (1 - c) * HALF, HALO + (1 - c) * HALF, HALF)
    if n2 > 1:
        low2 = v2w.at[pl.ds(0, HALO)]
        high2 = v2w.at[pl.ds(HALO + BLK, HALO)]
        up2 = remote(v2w.at[pl.ds(BLK, HALO)], low2, v2r_sem, 0, jnp.minimum(dom + 16, n_dom - 1))
        down2 = remote(v2w.at[pl.ds(HALO, HALO)], high2, v2r_sem, 1, jnp.maximum(dom - 16, 0))

        @pl.when(next2)
        def _():
            up2.start()

        @pl.when(prev2)
        def _():
            down2.start()

        @pl.when(prev2)
        def _():
            up2.wait_recv()
            maps(2, v2w, y2, 0, 0, HALO)

        @pl.when(next2)
        def _():
            down2.wait_recv()
            maps(2, v2w, y2, HALO + BLK, HALO + BLK, HALO)

        @pl.when(next2)
        def _():
            up2.wait_send()

        @pl.when(prev2)
        def _():
            down2.wait_send()

    def out_copy(i):
        return pltpu.make_async_copy(ob.at[pl.ds(2 * i, 2)], out_h.at[pl.ds(2 * i, 2)], out_sem.at[i])

    def finish(i, _):
        sides = near_pair(2, y2, nt, start2, start2, n_sub * BLK, i)
        for b, side in zip((2 * i, 2 * i + 1), sides):
            mid = u1[b] + dot(iw[1, mid_slot(zi, b)], side.astype(BF16))
            fine = u0[b] + dot(iw[0, fine_slot(dom, b)], mid.astype(BF16))
            ob[b] = gelu(fine).astype(BF16)
        out_copy(i).start()
        return 0

    lax.fori_loop(0, BLK // 2, finish, 0, unroll=True)

    core.wait_send()
    for copy in part + zsend + [v1x] + v1c + v2z + v2x + v2c:
        copy.wait_send()

    @pl.when(is_c1 & next1)
    def _():
        rim_up.wait_send()

    @pl.when(is_c0 & prev1)
    def _():
        rim_down.wait_send()

    @pl.when(is_c1 & prev1)
    def _():
        low_core.wait_send()

    @pl.when(is_c0 & next1)
    def _():
        high_core.wait_send()

    for i in range(BLK // 2):
        out_copy(i).wait()


def shards(n_dom, n_sub, feat, near_fine, near_mid, near_top, restrict_mid, restrict_top, *weights):
    lists = [x.T for x in (near_fine, near_mid, near_top, restrict_mid, restrict_top)]
    any_spec = pl.BlockSpec(memory_space=pl.ANY)
    wide = HALO + BLK + HALO
    dma = pltpu.SemaphoreType.DMA
    vmem = pltpu.VMEM
    smem = pltpu.SMEM
    blocks = lambda n, kind=BF16, width=C: vmem((n, BS, width), kind)
    scratch = [
        blocks(BLK),
        vmem((3, KN, BS, BS), BF16),
        vmem((3, KN, C, C), BF16),
        vmem((2, 4, BS, BS), BF16),
        vmem((2, 4, BS, BS), BF16),
        vmem((C, C), BF16),
        *(smem(x.shape, jnp.int32) for x in lists),
        blocks(2 * HALO),
        blocks(HALF),
        blocks(QTR),
        blocks(QTR, F32),
        blocks(QTR),
        blocks(wide),
        blocks(3),
        blocks(wide),
        blocks(wide, BF16, KN * C),
        blocks(wide, BF16, KN * C),
        blocks(wide, BF16, KN * C),
        blocks(BLK, F32),
        blocks(BLK, F32),
        blocks(BLK),
        dma((11,)),
        dma((BLK // 2,)),
        dma((2, 1)),
        dma((2, 2)),
        dma((2, 4)),
        dma((2, 3)),
        dma((2, 1)),
        dma((2, 2)),
        dma((2, 2)),
        dma((2, 2)),
        dma((2, 3)),
        dma((2, 4)),
        dma((2, 8)),
        dma((2, 2)),
    ]
    out = pl.pallas_call(
        functools.partial(kernel, n_dom, n_sub),
        out_shape=jax.ShapeDtypeStruct((BLK, BS, C), BF16),
        in_specs=[pl.BlockSpec(memory_space=pltpu.HBM)] * 11,
        out_specs=any_spec,
        scratch_shapes=scratch,
        compiler_params=pltpu.CompilerParams(
            collective_id=0, has_side_effects=True, vmem_limit_bytes=62 * 2**20
        ),
    )(feat.reshape(BLK, BS, C), *lists, *weights)
    return out.reshape(BLK * BS, C)


def solution(mesh):
    rows = P(("dom", "sub"), None)
    in_specs = (rows, rows) + (P(),) * 9
    inner = functools.partial(shards, mesh.shape["dom"], mesh.shape["sub"])
    return jax.shard_map(inner, mesh=mesh, in_specs=in_specs, out_specs=rows, check_vma=False)
```

```python
import functools

import jax
import jax.numpy as jnp
from jax import lax
from jax.experimental import pallas as pl
from jax.experimental.pallas import tpu as pltpu
from jax.sharding import PartitionSpec as P

C = 128
BS = 128
KN = 3
BLK = 16
HALO = 4
HALF = BLK // 2
QTR = BLK // 4
F32 = jnp.float32
BF16 = jnp.bfloat16
MESH = pl.DeviceIdType.MESH


def dot(a, b):
    return jnp.dot(a, b, preferred_element_type=F32)


def gelu(x):
    inner = 0.7978845608028654 * (x + 0.044715 * (x * x * x))
    return 0.5 * x * (1.0 + jnp.tanh(inner))


def kernel(
    n_dom,
    n_sub,
    feat_h,
    nf_h,
    nm_h,
    nt_h,
    rm_h,
    rt_h,
    nk_h,
    ck_h,
    rw_h,
    iw_h,
    sk_h,
    out_h,
    v0,
    nk,
    ck,
    rw,
    iw,
    sk,
    nf,
    nm,
    nt,
    rm,
    rt,
    h0,
    r1,
    ps,
    pf,
    pr,
    v1w,
    zr,
    v2w,
    y0,
    y1,
    y2,
    u0,
    u1,
    ob,
    in_sem,
    out_sem,
    core_sem,
    fine_sem,
    part_sem,
    zs_sem,
    v1x_sem,
    v1c_sem,
    rim_sem,
    rimc_sem,
    v2z_sem,
    v2x_sem,
    v2c_sem,
    v2r_sem,
):
    dom = lax.axis_index("dom")
    sub = lax.axis_index("sub")
    n1 = n_dom // 4
    n2 = n_dom // 16
    g1 = dom // 4
    g2 = dom // 16
    r = dom % 4
    c = r % 2
    xb = r // 2
    zi = g1 % 4
    core_dom = dom + 1 - 2 * c
    x_dom = dom + 2 - 4 * xb
    q0 = c * HALF + xb * QTR
    qx = c * HALF + (1 - xb) * QTR
    start0 = (dom * n_sub + sub) * BLK
    start1 = (g1 * n_sub + sub) * BLK
    start2 = (g2 * n_sub + sub) * BLK
    me = dom * n_sub + sub
    prev_ok = me > 0
    next_ok = me < n_dom * n_sub - 1
    prev_dom = (me + n_dom * n_sub - 1) % (n_dom * n_sub) // n_sub
    prev_sub = (sub + n_sub - 1) % n_sub
    next_dom = (me + 1) % (n_dom * n_sub) // n_sub
    next_sub = (sub + 1) % n_sub
    prev1 = g1 > 0
    next1 = g1 < n1 - 1
    prev2 = g2 > 0
    next2 = g2 < n2 - 1
    is_c1 = c == 1
    is_c0 = c == 0

    def z_dom(k):
        return dom + ((zi + k) % 4 - zi) * 4

    loads = [
        pltpu.make_async_copy(feat_h, v0, in_sem.at[0]),
        pltpu.make_async_copy(rw_h, rw, in_sem.at[1]),
        pltpu.make_async_copy(rm_h, rm, in_sem.at[2]),
        pltpu.make_async_copy(rt_h, rt, in_sem.at[3]),
        pltpu.make_async_copy(ck_h, ck, in_sem.at[4]),
        pltpu.make_async_copy(sk_h, sk, in_sem.at[5]),
        pltpu.make_async_copy(nf_h, nf, in_sem.at[6]),
        pltpu.make_async_copy(nm_h, nm, in_sem.at[7]),
        pltpu.make_async_copy(nt_h, nt, in_sem.at[8]),
        pltpu.make_async_copy(nk_h, nk, in_sem.at[9]),
        pltpu.make_async_copy(iw_h, iw, in_sem.at[10]),
    ]
    for copy in loads:
        copy.start()

    barrier = pltpu.get_barrier_semaphore()

    def greet(d, s):
        pl.semaphore_signal(barrier, inc=1, device_id={"dom": d, "sub": s}, device_id_type=MESH)

    greet(core_dom, sub)
    greet(x_dom, sub)
    for k in range(1, 4):
        greet(z_dom(k), sub)
    both = [
        (prev_ok, prev_dom, prev_sub),
        (next_ok, next_dom, next_sub),
    ]
    if n1 > 4:
        both += [(prev1, dom - 4, sub), (next1, dom + 4, sub)]
    if n2 > 1:
        both += [(prev2, dom - 16, sub), (next2, dom + 16, sub)]
    for ok, d, s in both:
        @pl.when(ok)
        def _(d=d, s=s):
            greet(d, s)
    expected = 5
    for ok, _, _ in both:
        expected = expected + jnp.where(ok, 1, 0)
    pl.semaphore_wait(barrier, expected)

    def remote(src, dst, sems, i, d, s=None):
        return pltpu.make_async_remote_copy(
            src_ref=src,
            dst_ref=dst,
            send_sem=sems.at[0, i],
            recv_sem=sems.at[1, i],
            device_id={"dom": d, "sub": sub if s is None else s},
            device_id_type=MESH,
        )

    def own_slot(kids, b, ident):
        s = jnp.where(kids[1, b] == ident, 1, 0)
        s = jnp.where(kids[2, b] == ident, 2, s)
        return jnp.where(kids[3, b] == ident, 3, s)

    def fine_slot(d, b):
        return own_slot(rm, start1 + b, (d * n_sub + sub) * BLK + b)

    def mid_slot(k, b):
        return own_slot(rt, start2 + b, ((g2 * 4 + k) * n_sub + sub) * BLK + b)

    def local(near, own, pitch):
        lower = near - (own - pitch) - (BLK - HALO)
        upper = near - (own + pitch) + HALO + BLK
        mine = near - own + HALO
        window = jnp.where(near < own, lower, jnp.where(near >= own + BLK, upper, mine))
        return jnp.clip(window, 0, BLK + 2 * HALO - 1)

    loads[0].wait()
    core = remote(v0.at[pl.ds((1 - c) * HALF, HALF)], r1, core_sem, 0, core_dom)
    core.start()
    up = remote(v0.at[pl.ds(BLK - HALO, HALO)], h0.at[pl.ds(0, HALO)], fine_sem, 0, next_dom, next_sub)
    down = remote(v0.at[pl.ds(0, HALO)], h0.at[pl.ds(HALO, HALO)], fine_sem, 1, prev_dom, prev_sub)

    for copy in loads[1:]:
        copy.wait()

    def maps(level, src, dst, first, at, count):
        wide = jnp.concatenate([ck[level, 0], ck[level, 1], ck[level, 2]], axis=1)
        rows = src[pl.ds(first, count)].reshape(count * BS, C)
        dst[pl.ds(at, count)] = dot(rows, wide).astype(BF16).reshape(count, BS, KN * C)

    def own_maps(i, _):
        rows = v0[pl.ds(i * 4, 4)].reshape(4 * BS, C)
        left = jnp.concatenate([ck[0, 0], ck[0, 1]], axis=1)
        right = jnp.concatenate([ck[0, 2], sk[...]], axis=1)
        y0[pl.ds(HALO + i * 4, 4), :, pl.ds(0, 2 * C)] = dot(rows, left).astype(BF16).reshape(4, BS, 2 * C)
        got = dot(rows, right)
        y0[pl.ds(HALO + i * 4, 4), :, pl.ds(2 * C, C)] = got[:, :C].astype(BF16).reshape(4, BS, C)
        u0[pl.ds(i * 4, 4)] = got[:, C:].reshape(4, BS, C)
        return 0

    lax.fori_loop(0, 4, own_maps, 0, unroll=True)

    core.wait_recv()

    def chip_sum(b):
        mats = jnp.concatenate([rw[0, fine_slot(dom, b)], rw[0, fine_slot(core_dom, b)]], axis=1)
        vals = jnp.concatenate([v0[b], r1[b - c * HALF]], axis=0)
        return dot(mats, vals)

    part = [remote(ps.at[i], pr.at[i], part_sem, i, x_dom) for i in range(QTR)]
    for i in range(QTR):
        ps[i] = chip_sum(qx + i).astype(BF16)
        part[i].start()
    for i in range(QTR):
        pf[i] = chip_sum(q0 + i)

    @pl.when(next_ok)
    def _():
        up.start()

    @pl.when(prev_ok)
    def _():
        down.start()

    def near_pair(level, y, near, first, own, pitch, i, cols):
        mats = jnp.concatenate([nk[level, k] for k in cols], axis=1)
        sides = []
        for b in (2 * i, 2 * i + 1):
            picks = [
                y[local(near[k, first + b], own, pitch), :, pl.ds(k * C, C)] for k in cols
            ]
            sides.append(jnp.concatenate(picks, axis=0))
        got = dot(mats, jnp.concatenate(sides, axis=1))
        return got[:, :C], got[:, C:]

    def near_fine(cols, i, _):
        one, two = near_pair(0, y0, nf, 0, start0, BLK, i, cols)
        u0[2 * i] += one
        u0[2 * i + 1] += two
        return 0

    lax.fori_loop(0, BLK // 2, functools.partial(near_fine, (0,)), 0, unroll=True)

    zsend = [
        remote(v1w.at[HALO + q0 + (zi + k) % 4], zr.at[k - 1], zs_sem, k - 1, z_dom(k))
        for k in range(1, 4)
    ]
    for i in range(QTR):
        part[i].wait_recv()
        v1w[HALO + q0 + i] = (pf[i] + pr[i].astype(F32)).astype(BF16)
    for copy in (zsend[1], zsend[0], zsend[2]):
        copy.start()
    own_quarter = v1w.at[pl.ds(HALO + q0, QTR)]
    other_quarter = v1w.at[pl.ds(HALO + qx, QTR)]
    v1x = remote(own_quarter, own_quarter, v1x_sem, 0, x_dom)
    v1x.start()
    v1c = [
        remote(own_quarter, own_quarter, v1c_sem, 0, core_dom),
        remote(other_quarter, other_quarter, v1c_sem, 1, core_dom),
    ]
    v1c[0].start()

    @pl.when(prev_ok)
    def _():
        down.wait_send()

    @pl.when(next_ok)
    def _():
        up.wait_send()

    @pl.when(prev_ok)
    def _():
        up.wait_recv()
        rows = h0[pl.ds(0, HALO)].reshape(HALO * BS, C)
        y0[pl.ds(0, HALO), :, pl.ds(C, C)] = dot(rows, ck[0, 1]).astype(BF16).reshape(HALO, BS, C)

    @pl.when(next_ok)
    def _():
        down.wait_recv()
        rows = h0[pl.ds(HALO, HALO)].reshape(HALO * BS, C)
        y0[pl.ds(HALO + BLK, HALO), :, pl.ds(2 * C, C)] = dot(rows, ck[0, 2]).astype(BF16).reshape(HALO, BS, C)

    lax.fori_loop(0, BLK // 2, functools.partial(near_fine, (1, 2)), 0, unroll=True)

    b2 = q0 + zi
    mine = dot(rw[1, mid_slot(zi, b2)], v1w[HALO + b2])
    for copy in zsend:
        copy.wait_recv()
    mats = [rw[1, mid_slot((zi + 4 - k) % 4, b2)] for k in range(1, 4)]
    vals = [zr[k - 1] for k in range(1, 4)]
    mine = mine + dot(jnp.concatenate(mats, axis=1), jnp.concatenate(vals, axis=0))
    v2w[HALO + b2] = mine.astype(BF16)

    def block2(b):
        return v2w.at[HALO + b]

    v2z = [remote(block2(b2), block2(b2), v2z_sem, k - 1, z_dom(k)) for k in range(1, 4)]
    for copy in (v2z[1], v2z[0], v2z[2]):
        copy.start()
    hops = [(zi + 4 - k) % 4 for k in range(4)]
    v2x = [remote(block2(q0 + h), block2(q0 + h), v2x_sem, k, x_dom) for k, h in enumerate(hops)]
    v2c = [remote(block2(q0 + h), block2(q0 + h), v2c_sem, k, core_dom) for k, h in enumerate(hops)]
    v2c += [remote(block2(qx + h), block2(qx + h), v2c_sem, 4 + k, core_dom) for k, h in enumerate(hops)]
    v2x[0].start()
    v2c[0].start()

    v1x.wait_recv()
    v1c[1].start()
    low = v1w.at[pl.ds(0, HALO)]
    high = v1w.at[pl.ds(HALO + BLK, HALO)]
    rim_up = remote(v1w.at[pl.ds(BLK, HALO)], low, rim_sem, 0, jnp.minimum(dom + 4, n_dom - 1))
    rim_down = remote(v1w.at[pl.ds(HALO, HALO)], high, rim_sem, 1, jnp.maximum(dom - 4, 0))
    low_core = remote(low, low, rimc_sem, 0, core_dom)
    high_core = remote(high, high, rimc_sem, 1, core_dom)

    @pl.when(is_c1 & next1)
    def _():
        rim_up.start()

    @pl.when(is_c0 & prev1)
    def _():
        rim_down.start()

    v1c[0].wait_recv()
    v1c[1].wait_recv()

    def mid_maps(i, _):
        maps(1, v1w, y1, HALO + i * 4, HALO + i * 4, 4)
        return 0

    lax.fori_loop(0, 4, mid_maps, 0, unroll=True)

    def near_mid_own(i, _):
        u1[2 * i], u1[2 * i + 1] = near_pair(1, y1, nm, start1, start1, n_sub * BLK, i, (0,))
        return 0

    lax.fori_loop(0, BLK // 2, near_mid_own, 0, unroll=True)

    for k in (1, 3, 2):
        v2z[k - 1].wait_recv()
        v2x[k].start()
        v2c[k].start()

    @pl.when(is_c1 & prev1)
    def _():
        rim_up.wait_recv()
        low_core.start()

    @pl.when(is_c0 & next1)
    def _():
        rim_down.wait_recv()
        high_core.start()

    def rim_maps(at, k):
        rows = v1w[pl.ds(at, HALO)].reshape(HALO * BS, C)
        y1[pl.ds(at, HALO), :, pl.ds(k * C, C)] = dot(rows, ck[1, k]).astype(BF16).reshape(HALO, BS, C)

    @pl.when(prev1)
    def _():
        @pl.when(is_c0)
        def _():
            low_core.wait_recv()

        rim_maps(0, 1)

    @pl.when(next1)
    def _():
        @pl.when(is_c1)
        def _():
            high_core.wait_recv()

        rim_maps(HALO + BLK, 2)

    def near_mid_rims(i, _):
        one, two = near_pair(1, y1, nm, start1, start1, n_sub * BLK, i, (1, 2))
        u1[2 * i] += one
        u1[2 * i + 1] += two
        return 0

    for k in (0, 1, 3, 2):
        v2x[k].wait_recv()
        v2c[4 + k].start()
    lax.fori_loop(0, BLK // 2, near_mid_rims, 0, unroll=True)

    maps(2, v2w, y2, HALO + c * HALF, HALO + c * HALF, HALF)
    for k in range(2 * QTR):
        v2c[k].wait_recv()
    maps(2, v2w, y2, HALO + (1 - c) * HALF, HALO + (1 - c) * HALF, HALF)
    if n2 > 1:
        low2 = v2w.at[pl.ds(0, HALO)]
        high2 = v2w.at[pl.ds(HALO + BLK, HALO)]
        up2 = remote(v2w.at[pl.ds(BLK, HALO)], low2, v2r_sem, 0, jnp.minimum(dom + 16, n_dom - 1))
        down2 = remote(v2w.at[pl.ds(HALO, HALO)], high2, v2r_sem, 1, jnp.maximum(dom - 16, 0))

        @pl.when(next2)
        def _():
            up2.start()

        @pl.when(prev2)
        def _():
            down2.start()

        @pl.when(prev2)
        def _():
            up2.wait_recv()
            maps(2, v2w, y2, 0, 0, HALO)

        @pl.when(next2)
        def _():
            down2.wait_recv()
            maps(2, v2w, y2, HALO + BLK, HALO + BLK, HALO)

        @pl.when(next2)
        def _():
            up2.wait_send()

        @pl.when(prev2)
        def _():
            down2.wait_send()

    def out_copy(i):
        return pltpu.make_async_copy(ob.at[pl.ds(4 * i, 4)], out_h.at[pl.ds(4 * i, 4)], out_sem.at[i])

    def finish(i, _):
        pairs = (2 * i, 2 * i + 1)
        blks = [4 * i + n for n in range(4)]
        sides = sum((near_pair(2, y2, nt, start2, start2, n_sub * BLK, j, (0, 1, 2)) for j in pairs), ())
        sides = [side.astype(BF16) for side in sides]
        mids = [u1[b] + dot(iw[1, mid_slot(zi, b)], side) for b, side in zip(blks, sides)]
        mids = [mid.astype(BF16) for mid in mids]
        fines = [u0[b] + dot(iw[0, fine_slot(dom, b)], mid) for b, mid in zip(blks, mids)]
        for b, fine in zip(blks, fines):
            ob[b] = gelu(fine).astype(BF16)
        out_copy(i).start()
        return 0

    lax.fori_loop(0, BLK // 4, finish, 0, unroll=True)

    core.wait_send()
    for copy in part + zsend + [v1x] + v1c + v2z + v2x + v2c:
        copy.wait_send()

    @pl.when(is_c1 & next1)
    def _():
        rim_up.wait_send()

    @pl.when(is_c0 & prev1)
    def _():
        rim_down.wait_send()

    @pl.when(is_c1 & prev1)
    def _():
        low_core.wait_send()

    @pl.when(is_c0 & next1)
    def _():
        high_core.wait_send()

    for i in range(BLK // 4):
        out_copy(i).wait()


def shards(n_dom, n_sub, feat, near_fine, near_mid, near_top, restrict_mid, restrict_top, *weights):
    lists = [x.T for x in (near_fine, near_mid, near_top, restrict_mid, restrict_top)]
    any_spec = pl.BlockSpec(memory_space=pl.ANY)
    wide = HALO + BLK + HALO
    dma = pltpu.SemaphoreType.DMA
    vmem = pltpu.VMEM
    smem = pltpu.SMEM
    blocks = lambda n, kind=BF16, width=C: vmem((n, BS, width), kind)
    scratch = [
        blocks(BLK),
        vmem((3, KN, BS, BS), BF16),
        vmem((3, KN, C, C), BF16),
        vmem((2, 4, BS, BS), BF16),
        vmem((2, 4, BS, BS), BF16),
        vmem((C, C), BF16),
        *(smem(x.shape, jnp.int32) for x in lists),
        blocks(2 * HALO),
        blocks(HALF),
        blocks(QTR),
        blocks(QTR, F32),
        blocks(QTR),
        blocks(wide),
        blocks(3),
        blocks(wide),
        blocks(wide, BF16, KN * C),
        blocks(wide, BF16, KN * C),
        blocks(wide, BF16, KN * C),
        blocks(BLK, F32),
        blocks(BLK, F32),
        blocks(BLK),
        dma((11,)),
        dma((BLK // 4,)),
        dma((2, 1)),
        dma((2, 2)),
        dma((2, 4)),
        dma((2, 3)),
        dma((2, 1)),
        dma((2, 2)),
        dma((2, 2)),
        dma((2, 2)),
        dma((2, 3)),
        dma((2, 4)),
        dma((2, 8)),
        dma((2, 2)),
    ]
    out = pl.pallas_call(
        functools.partial(kernel, n_dom, n_sub),
        out_shape=jax.ShapeDtypeStruct((BLK, BS, C), BF16),
        in_specs=[pl.BlockSpec(memory_space=pltpu.HBM)] * 11,
        out_specs=any_spec,
        scratch_shapes=scratch,
        compiler_params=pltpu.CompilerParams(
            collective_id=0, has_side_effects=True, vmem_limit_bytes=62 * 2**20
        ),
    )(feat.reshape(BLK, BS, C), *lists, *weights)
    return out.reshape(BLK * BS, C)


def solution(mesh):
    rows = P(("dom", "sub"), None)
    in_specs = (rows, rows) + (P(),) * 9
    inner = functools.partial(shards, mesh.shape["dom"], mesh.shape["sub"])
    return jax.shard_map(inner, mesh=mesh, in_specs=in_specs, out_specs=rows, check_vma=False)
```

```python
import functools

import jax
import jax.numpy as jnp
from jax import lax
from jax.experimental import pallas as pl
from jax.experimental.pallas import tpu as pltpu
from jax.sharding import PartitionSpec as P

C = 128
BS = 128
KN = 3
BLK = 16
HALO = 4
HALF = BLK // 2
QTR = BLK // 4
F32 = jnp.float32
BF16 = jnp.bfloat16
MESH = pl.DeviceIdType.MESH


def dot(a, b):
    return jnp.dot(a, b, preferred_element_type=F32)


def gelu(x):
    inner = 0.7978845608028654 * (x + 0.044715 * (x * x * x))
    return 0.5 * x * (1.0 + jnp.tanh(inner))


def kernel(
    n_dom,
    n_sub,
    feat_h,
    nf_h,
    nm_h,
    nt_h,
    rm_h,
    rt_h,
    nk_h,
    ck_h,
    rw_h,
    iw_h,
    sk_h,
    out,
    v0,
    nk,
    ck,
    rw,
    iw,
    sk,
    nf,
    nm,
    nt,
    rm,
    rt,
    h0,
    r1,
    ps,
    pf,
    pr,
    v1w,
    zr,
    v2w,
    y0,
    y1,
    y2,
    u0,
    u1,
    in_sem,
    core_sem,
    fine_sem,
    part_sem,
    zs_sem,
    v1x_sem,
    v1c_sem,
    rim_sem,
    rimc_sem,
    v2z_sem,
    v2x_sem,
    v2c_sem,
    v2r_sem,
):
    dom = lax.axis_index("dom")
    sub = lax.axis_index("sub")
    n1 = n_dom // 4
    n2 = n_dom // 16
    g1 = dom // 4
    g2 = dom // 16
    r = dom % 4
    c = r % 2
    xb = r // 2
    zi = g1 % 4
    core_dom = dom + 1 - 2 * c
    x_dom = dom + 2 - 4 * xb
    q0 = c * HALF + xb * QTR
    qx = c * HALF + (1 - xb) * QTR
    start0 = (dom * n_sub + sub) * BLK
    start1 = (g1 * n_sub + sub) * BLK
    start2 = (g2 * n_sub + sub) * BLK
    me = dom * n_sub + sub
    prev_ok = me > 0
    next_ok = me < n_dom * n_sub - 1
    prev_dom = (me + n_dom * n_sub - 1) % (n_dom * n_sub) // n_sub
    prev_sub = (sub + n_sub - 1) % n_sub
    next_dom = (me + 1) % (n_dom * n_sub) // n_sub
    next_sub = (sub + 1) % n_sub
    prev1 = g1 > 0
    next1 = g1 < n1 - 1
    prev2 = g2 > 0
    next2 = g2 < n2 - 1
    is_c1 = c == 1
    is_c0 = c == 0

    def z_dom(k):
        return dom + ((zi + k) % 4 - zi) * 4

    loads = [
        pltpu.make_async_copy(feat_h, v0, in_sem.at[0]),
        pltpu.make_async_copy(rw_h, rw, in_sem.at[1]),
        pltpu.make_async_copy(rm_h, rm, in_sem.at[2]),
        pltpu.make_async_copy(rt_h, rt, in_sem.at[3]),
        pltpu.make_async_copy(ck_h, ck, in_sem.at[4]),
        pltpu.make_async_copy(sk_h, sk, in_sem.at[5]),
        pltpu.make_async_copy(nf_h, nf, in_sem.at[6]),
        pltpu.make_async_copy(nm_h, nm, in_sem.at[7]),
        pltpu.make_async_copy(nt_h, nt, in_sem.at[8]),
        pltpu.make_async_copy(nk_h, nk, in_sem.at[9]),
        pltpu.make_async_copy(iw_h, iw, in_sem.at[10]),
    ]
    for copy in loads:
        copy.start()

    barrier = pltpu.get_barrier_semaphore()

    def greet(d, s):
        pl.semaphore_signal(barrier, inc=1, device_id={"dom": d, "sub": s}, device_id_type=MESH)

    greet(core_dom, sub)
    greet(x_dom, sub)
    for k in range(1, 4):
        greet(z_dom(k), sub)
    both = [
        (prev_ok, prev_dom, prev_sub),
        (next_ok, next_dom, next_sub),
    ]
    if n1 > 4:
        both += [(prev1, dom - 4, sub), (next1, dom + 4, sub)]
    if n2 > 1:
        both += [(prev2, dom - 16, sub), (next2, dom + 16, sub)]
    for ok, d, s in both:
        @pl.when(ok)
        def _(d=d, s=s):
            greet(d, s)
    expected = 5
    for ok, _, _ in both:
        expected = expected + jnp.where(ok, 1, 0)
    pl.semaphore_wait(barrier, expected)

    def remote(src, dst, sems, i, d, s=None):
        return pltpu.make_async_remote_copy(
            src_ref=src,
            dst_ref=dst,
            send_sem=sems.at[0, i],
            recv_sem=sems.at[1, i],
            device_id={"dom": d, "sub": sub if s is None else s},
            device_id_type=MESH,
        )

    def own_slot(kids, b, ident):
        s = jnp.where(kids[1, b] == ident, 1, 0)
        s = jnp.where(kids[2, b] == ident, 2, s)
        return jnp.where(kids[3, b] == ident, 3, s)

    def fine_slot(d, b):
        return own_slot(rm, start1 + b, (d * n_sub + sub) * BLK + b)

    def mid_slot(k, b):
        return own_slot(rt, start2 + b, ((g2 * 4 + k) * n_sub + sub) * BLK + b)

    def local(near, own, pitch):
        lower = near - (own - pitch) - (BLK - HALO)
        upper = near - (own + pitch) + HALO + BLK
        mine = near - own + HALO
        window = jnp.where(near < own, lower, jnp.where(near >= own + BLK, upper, mine))
        return jnp.clip(window, 0, BLK + 2 * HALO - 1)

    loads[0].wait()
    core = []
    for i, at in enumerate(((1 - xb) * QTR, xb * QTR)):
        core.append(
            remote(
                v0.at[pl.ds((1 - c) * HALF + at, QTR)], r1.at[pl.ds(at, QTR)], core_sem, i, core_dom
            )
        )
        core[i].start()
    up = remote(v0.at[pl.ds(BLK - HALO, HALO)], h0.at[pl.ds(0, HALO)], fine_sem, 0, next_dom, next_sub)
    down = remote(v0.at[pl.ds(0, HALO)], h0.at[pl.ds(HALO, HALO)], fine_sem, 1, prev_dom, prev_sub)

    for copy in loads[1:]:
        copy.wait()

    def maps(level, src, dst, first, at, count):
        wide = jnp.concatenate([ck[level, 0], ck[level, 1], ck[level, 2]], axis=1)
        rows = src[pl.ds(first, count)].reshape(count * BS, C)
        dst[pl.ds(at, count)] = dot(rows, wide).astype(BF16).reshape(count, BS, KN * C)

    def own_maps(i, _):
        rows = v0[pl.ds(i * 4, 4)].reshape(4 * BS, C)
        left = jnp.concatenate([ck[0, 0], ck[0, 1]], axis=1)
        right = jnp.concatenate([ck[0, 2], sk[...]], axis=1)
        y0[pl.ds(HALO + i * 4, 4), :, pl.ds(0, 2 * C)] = dot(rows, left).astype(BF16).reshape(4, BS, 2 * C)
        got = dot(rows, right)
        y0[pl.ds(HALO + i * 4, 4), :, pl.ds(2 * C, C)] = got[:, :C].astype(BF16).reshape(4, BS, C)
        u0[pl.ds(i * 4, 4)] = got[:, C:].reshape(4, BS, C)
        return 0

    lax.fori_loop(0, 4, own_maps, 0, unroll=True)

    core[0].wait_recv()

    def chip_sum(b):
        mats = jnp.concatenate([rw[0, fine_slot(dom, b)], rw[0, fine_slot(core_dom, b)]], axis=1)
        vals = jnp.concatenate([v0[b], r1[b - c * HALF]], axis=0)
        return dot(mats, vals)

    order = (2, 1, 3, 0)
    turn = [(zi + k) % 4 for k in range(4)]
    part = [remote(ps.at[k], pr.at[k], part_sem, k, x_dom) for k in range(QTR)]
    for k in order:
        ps[k] = chip_sum(qx + turn[k]).astype(BF16)
        part[k].start()
    core[1].wait_recv()
    for k in order:
        pf[k] = chip_sum(q0 + turn[k])

    def near_pair(level, y, near, first, own, pitch, i, cols):
        mats = jnp.concatenate([nk[level, k] for k in cols], axis=1)
        sides = []
        for b in (2 * i, 2 * i + 1):
            picks = [
                y[local(near[k, first + b], own, pitch), :, pl.ds(k * C, C)] for k in cols
            ]
            sides.append(jnp.concatenate(picks, axis=0))
        got = dot(mats, jnp.concatenate(sides, axis=1))
        return got[:, :C], got[:, C:]

    def near_fine(cols, i, _):
        one, two = near_pair(0, y0, nf, 0, start0, BLK, i, cols)
        u0[2 * i] += one
        u0[2 * i + 1] += two
        return 0

    lax.fori_loop(0, BLK // 2, functools.partial(near_fine, (0,)), 0, unroll=True)

    zsend = [
        remote(v1w.at[HALO + q0 + turn[k]], zr.at[k - 1], zs_sem, k - 1, z_dom(k))
        for k in range(1, 4)
    ]
    for k in order:
        part[k].wait_recv()
        v1w[HALO + q0 + turn[k]] = (pf[k] + pr[k].astype(F32)).astype(BF16)
        if k:
            zsend[k - 1].start()
    own_quarter = v1w.at[pl.ds(HALO + q0, QTR)]
    other_quarter = v1w.at[pl.ds(HALO + qx, QTR)]
    v1x = remote(own_quarter, own_quarter, v1x_sem, 0, x_dom)
    v1x.start()
    v1c = [
        remote(own_quarter, own_quarter, v1c_sem, 0, core_dom),
        remote(other_quarter, other_quarter, v1c_sem, 1, core_dom),
    ]
    v1c[0].start()

    @pl.when(next_ok)
    def _():
        up.start()

    @pl.when(prev_ok)
    def _():
        down.start()

    b2 = q0 + zi
    mine = dot(rw[1, mid_slot(zi, b2)], v1w[HALO + b2])
    for copy in zsend:
        copy.wait_recv()
    mats = [rw[1, mid_slot((zi + 4 - k) % 4, b2)] for k in range(1, 4)]
    vals = [zr[k - 1] for k in range(1, 4)]
    mine = mine + dot(jnp.concatenate(mats, axis=1), jnp.concatenate(vals, axis=0))
    v2w[HALO + b2] = mine.astype(BF16)

    def block2(b):
        return v2w.at[HALO + b]

    v2z = [remote(block2(b2), block2(b2), v2z_sem, k - 1, z_dom(k)) for k in range(1, 4)]
    for copy in (v2z[1], v2z[0], v2z[2]):
        copy.start()
    hops = [(zi + 4 - k) % 4 for k in range(4)]
    v2x = [remote(block2(q0 + h), block2(q0 + h), v2x_sem, k, x_dom) for k, h in enumerate(hops)]
    v2c = [remote(block2(q0 + h), block2(q0 + h), v2c_sem, k, core_dom) for k, h in enumerate(hops)]
    v2c += [remote(block2(qx + h), block2(qx + h), v2c_sem, 4 + k, core_dom) for k, h in enumerate(hops)]
    v2x[0].start()
    v2c[0].start()

    v1x.wait_recv()
    v1c[1].start()
    low = v1w.at[pl.ds(0, HALO)]
    high = v1w.at[pl.ds(HALO + BLK, HALO)]
    rim_up = remote(v1w.at[pl.ds(BLK, HALO)], low, rim_sem, 0, jnp.minimum(dom + 4, n_dom - 1))
    rim_down = remote(v1w.at[pl.ds(HALO, HALO)], high, rim_sem, 1, jnp.maximum(dom - 4, 0))
    low_core = remote(low, low, rimc_sem, 0, core_dom)
    high_core = remote(high, high, rimc_sem, 1, core_dom)

    @pl.when(is_c1 & next1)
    def _():
        rim_up.start()

    @pl.when(is_c0 & prev1)
    def _():
        rim_down.start()

    v1c[0].wait_recv()
    v1c[1].wait_recv()

    def mid_maps(i, _):
        maps(1, v1w, y1, HALO + i * 4, HALO + i * 4, 4)
        return 0

    lax.fori_loop(0, 4, mid_maps, 0, unroll=True)

    def near_mid_own(i, _):
        u1[2 * i], u1[2 * i + 1] = near_pair(1, y1, nm, start1, start1, n_sub * BLK, i, (0,))
        return 0

    lax.fori_loop(0, BLK // 2, near_mid_own, 0, unroll=True)

    for k in (1, 3, 2):
        v2z[k - 1].wait_recv()
        v2x[k].start()
        v2c[k].start()

    @pl.when(is_c1 & prev1)
    def _():
        rim_up.wait_recv()
        low_core.start()

    @pl.when(is_c0 & next1)
    def _():
        rim_down.wait_recv()
        high_core.start()

    def rim_maps(at, k):
        rows = v1w[pl.ds(at, HALO)].reshape(HALO * BS, C)
        y1[pl.ds(at, HALO), :, pl.ds(k * C, C)] = dot(rows, ck[1, k]).astype(BF16).reshape(HALO, BS, C)

    @pl.when(prev1)
    def _():
        @pl.when(is_c0)
        def _():
            low_core.wait_recv()

        rim_maps(0, 1)

    @pl.when(next1)
    def _():
        @pl.when(is_c1)
        def _():
            high_core.wait_recv()

        rim_maps(HALO + BLK, 2)

    def near_mid_rims(i, _):
        one, two = near_pair(1, y1, nm, start1, start1, n_sub * BLK, i, (1, 2))
        u1[2 * i] += one
        u1[2 * i + 1] += two
        return 0

    @pl.when(prev_ok)
    def _():
        down.wait_send()

    @pl.when(next_ok)
    def _():
        up.wait_send()

    @pl.when(prev_ok)
    def _():
        up.wait_recv()
        rows = h0[pl.ds(0, HALO)].reshape(HALO * BS, C)
        y0[pl.ds(0, HALO), :, pl.ds(C, C)] = dot(rows, ck[0, 1]).astype(BF16).reshape(HALO, BS, C)

    @pl.when(next_ok)
    def _():
        down.wait_recv()
        rows = h0[pl.ds(HALO, HALO)].reshape(HALO * BS, C)
        y0[pl.ds(HALO + BLK, HALO), :, pl.ds(2 * C, C)] = dot(rows, ck[0, 2]).astype(BF16).reshape(HALO, BS, C)

    for k in (0, 1, 3, 2):
        v2x[k].wait_recv()
        v2c[4 + k].start()
    lax.fori_loop(0, BLK // 2, near_mid_rims, 0, unroll=True)
    lax.fori_loop(0, BLK // 2, functools.partial(near_fine, (1, 2)), 0, unroll=True)

    maps(2, v2w, y2, HALO + c * HALF, HALO + c * HALF, HALF)
    for k in range(2 * QTR):
        v2c[k].wait_recv()
    maps(2, v2w, y2, HALO + (1 - c) * HALF, HALO + (1 - c) * HALF, HALF)
    if n2 > 1:
        low2 = v2w.at[pl.ds(0, HALO)]
        high2 = v2w.at[pl.ds(HALO + BLK, HALO)]
        up2 = remote(v2w.at[pl.ds(BLK, HALO)], low2, v2r_sem, 0, jnp.minimum(dom + 16, n_dom - 1))
        down2 = remote(v2w.at[pl.ds(HALO, HALO)], high2, v2r_sem, 1, jnp.maximum(dom - 16, 0))

        @pl.when(next2)
        def _():
            up2.start()

        @pl.when(prev2)
        def _():
            down2.start()

        @pl.when(prev2)
        def _():
            up2.wait_recv()
            maps(2, v2w, y2, 0, 0, HALO)

        @pl.when(next2)
        def _():
            down2.wait_recv()
            maps(2, v2w, y2, HALO + BLK, HALO + BLK, HALO)

        @pl.when(next2)
        def _():
            up2.wait_send()

        @pl.when(prev2)
        def _():
            down2.wait_send()

    def finish(i, _):
        pairs = (2 * i, 2 * i + 1)
        blks = [4 * i + n for n in range(4)]
        sides = sum((near_pair(2, y2, nt, start2, start2, n_sub * BLK, j, (0, 1, 2)) for j in pairs), ())
        sides = [side.astype(BF16) for side in sides]
        mids = [u1[b] + dot(iw[1, mid_slot(zi, b)], side) for b, side in zip(blks, sides)]
        mids = [mid.astype(BF16) for mid in mids]
        fines = [u0[b] + dot(iw[0, fine_slot(dom, b)], mid) for b, mid in zip(blks, mids)]
        for b, fine in zip(blks, fines):
            out[b] = gelu(fine).astype(BF16)
        return 0

    lax.fori_loop(0, BLK // 4, finish, 0, unroll=True)

    for copy in core + part + zsend + [v1x] + v1c + v2z + v2x + v2c:
        copy.wait_send()

    @pl.when(is_c1 & next1)
    def _():
        rim_up.wait_send()

    @pl.when(is_c0 & prev1)
    def _():
        rim_down.wait_send()

    @pl.when(is_c1 & prev1)
    def _():
        low_core.wait_send()

    @pl.when(is_c0 & next1)
    def _():
        high_core.wait_send()


def shards(n_dom, n_sub, feat, near_fine, near_mid, near_top, restrict_mid, restrict_top, *weights):
    lists = [x.T for x in (near_fine, near_mid, near_top, restrict_mid, restrict_top)]
    wide = HALO + BLK + HALO
    dma = pltpu.SemaphoreType.DMA
    vmem = pltpu.VMEM
    smem = pltpu.SMEM
    blocks = lambda n, kind=BF16, width=C: vmem((n, BS, width), kind)
    scratch = [
        blocks(BLK),
        vmem((3, KN, BS, BS), BF16),
        vmem((3, KN, C, C), BF16),
        vmem((2, 4, BS, BS), BF16),
        vmem((2, 4, BS, BS), BF16),
        vmem((C, C), BF16),
        *(smem(x.shape, jnp.int32) for x in lists),
        blocks(2 * HALO),
        blocks(HALF),
        blocks(QTR),
        blocks(QTR, F32),
        blocks(QTR),
        blocks(wide),
        blocks(3),
        blocks(wide),
        blocks(wide, BF16, KN * C),
        blocks(wide, BF16, KN * C),
        blocks(wide, BF16, KN * C),
        blocks(BLK, F32),
        blocks(BLK, F32),
        dma((11,)),
        dma((2, 2)),
        dma((2, 2)),
        dma((2, 4)),
        dma((2, 3)),
        dma((2, 1)),
        dma((2, 2)),
        dma((2, 2)),
        dma((2, 2)),
        dma((2, 3)),
        dma((2, 4)),
        dma((2, 8)),
        dma((2, 2)),
    ]
    out = pl.pallas_call(
        functools.partial(kernel, n_dom, n_sub),
        out_shape=pltpu.VMEM((BLK, BS, C), BF16),
        in_specs=[pl.BlockSpec(memory_space=pltpu.HBM)] * 11,
        out_specs=pl.BlockSpec(memory_space=pltpu.VMEM),
        scratch_shapes=scratch,
        compiler_params=pltpu.CompilerParams(
            collective_id=0, has_side_effects=True, vmem_limit_bytes=62 * 2**20
        ),
    )(feat.reshape(BLK, BS, C), *lists, *weights)
    return out.reshape(BLK * BS, C)


def solution(mesh):
    rows = P(("dom", "sub"), None)
    in_specs = (rows, rows) + (P(),) * 9
    inner = functools.partial(shards, mesh.shape["dom"], mesh.shape["sub"])
    return jax.shard_map(inner, mesh=mesh, in_specs=in_specs, out_specs=rows, check_vma=False)
```
